256 devices in a mesh: dp: 4 (over y_hi, core), mp: 64 (over y_lo, x, z).
Axes of the slice: x: 4, y: 4 (y_hi: 2, y_lo: 2; y = y_hi * 2 + y_lo), z: 8, core: 2. Of those that a mesh axis runs over, the one named last changes fastest.
Arguments:
- patches: bfloat16 [1024, 6144], P('dp', 'mp'), may hold values from -110 to 110, as said below
- proj_in: bfloat16 [6144, 24576], P(None, 'mp'), may hold values from -0.21875 to 0.21875
- proj_out: bfloat16 [24576, 6144], P('mp'), may hold values from -0.109375 to 0.109375
- cotangent: bfloat16 [1024, 6144], P('dp', 'mp'), may hold values from -6 to 6
Outputs:
- mlp_out: bfloat16 [1024, 6144], P('dp', 'mp')
- patch_grad: bfloat16 [1024, 6144], P('dp', 'mp')
- grad_in: bfloat16 [6144, 24576], P('dp', 'mp')
- grad_out: bfloat16 [24576, 6144], P('mp', 'dp')
The draws below stay inside these ranges and needn't reach their ends.
Inputs may be any that keep to these rules, and one draw needn't show every extreme that they name: `patches`: Real-valued activations whose rows and features have differing scales.
All inputs are finite; a program needn't handle non-finite values.
Results may differ from the reference program's by a relative error of at most 0.012.
Values may be sent and summed in bfloat16 or wider, within the bound.
No kernel may reach another device: no remote copies, remote signals or barrier semaphores. Data moves between devices by JAX's collectives and lax.ppermute only.
A program may use at most 192 MiB of HBM per device.

```python
import jax
import jax.numpy as jnp
from jax import lax

D = 6144
FF = 24576
TOK_DEV = 256
TOKENS = 1024
N_DP = 4


def draw_patches(key, part):
    key = jax.random.fold_in(key, 11)
    key_base, key_rows, key_cols = jax.random.split(key, 3)
    ramp = jnp.power(3.0, jnp.arange(D, dtype=jnp.float32) / (D - 1)) / 1.7
    base = jnp.clip(jax.random.normal(key_base, (TOKENS, D), jnp.float32), -6.0, 6.0)
    row_scale = jnp.power(10.0, jax.random.uniform(key_rows, (TOKENS, 1), jnp.float32, -0.5, 0.5))
    col_scale = ramp * jnp.power(10.0, jax.random.uniform(key_cols, (1, D), jnp.float32, -0.5, 0.5))
    return (base * row_scale * col_scale).astype(jnp.bfloat16)


def raised(values, own_key, source, target, shards_of, factor):
    owner, partner = [(jnp.arange(values.shape[axis_at]) // (values.shape[axis_at] // shards_of)).reshape([-1 if axis == axis_at else 1 for axis in range(values.ndim)]) for axis_at in (source, target)]
    chosen = jax.random.permutation(own_key, shards_of)[partner]
    strong = (owner == chosen) | (owner == (partner + shards_of // 2) % shards_of)
    return jnp.where(strong, factor * values, values)


def levels(rng, dims, shards, least, largest):
    gain, own = 1.0, jax.random.fold_in(rng, 6)
    for axis_at, blocks in shards:
        steps = jnp.exp(jax.random.uniform(jax.random.fold_in(own, axis_at), (blocks,), jnp.float32, least / len(shards), largest / len(shards)))
        gain = gain * jnp.repeat(steps, dims[axis_at] // blocks).reshape([-1 if axis == axis_at else 1 for axis in range(len(dims))])
    return gain


def noise(own_key, shape, deviation, limit, shards=(), kind=jnp.bfloat16):
    loudness = levels(own_key, shape, shards, -0.22, 0.18) if shards else 1.0
    array = jax.random.normal(own_key, shape, jnp.float32) * deviation * loudness
    return jnp.minimum(jnp.maximum(array, -limit), limit).astype(kind)


def gaussian_with(own_key, extent, width, bound, shards, heavy, kind=jnp.bfloat16):
    values = width * jax.random.normal(own_key, extent, jnp.float32)
    if shards:
        values = values * levels(own_key, extent, shards, -0.22, 0.18)
    return jnp.clip(raised(values, jax.random.fold_in(own_key, 3), *heavy), -bound, bound).astype(kind)


def setup_inputs(seed: int = 0) -> dict:
    arg_keys = jax.random.split(jax.random.key(seed), 5)
    return {
        "patches": draw_patches(jax.random.fold_in(arg_keys[4], 71), 0),
        "proj_in": gaussian_with(arg_keys[1], (D, FF), D ** -0.5, 0.21875, ((1, 64),), (1, 0, 64, 4.0)),
        "proj_out": gaussian_with(arg_keys[2], (FF, D), FF ** -0.5, 0.109375, ((0, 64),), (0, 1, 64, 4.0)),
        "cotangent": noise(arg_keys[3], (TOKENS, D), 1.0, 6.0, ((0, 4), (1, 64))),
    }


eps = 1e-06

def gelu_back(hidden_pre, grad_act):
    return jax.vjp(lambda values: jax.nn.gelu(values, approximate=True), hidden_pre)[1](grad_act)[0]

def rounded(values):
    low = lax.optimization_barrier(values.astype(jnp.bfloat16))
    return low.astype(jnp.float32)

def reference(patches, proj_in, proj_out, cotangent):
    wide_x = patches.astype(jnp.float32)
    row_mean = lax.optimization_barrier(jnp.mean(wide_x, axis=1, keepdims=True))
    row_var = lax.optimization_barrier(jnp.mean(wide_x * wide_x, axis=1, keepdims=True)) - row_mean * row_mean
    row_rstd = lax.rsqrt(row_var + eps)
    normed = (wide_x - row_mean) * row_rstd
    normed_low = normed.astype(jnp.bfloat16)
    hidden_pre = jnp.dot(normed_low, proj_in, preferred_element_type=jnp.float32)
    activated = jax.nn.gelu(hidden_pre, approximate=True).astype(jnp.bfloat16)
    mlp_out = jnp.dot(activated, proj_out, preferred_element_type=jnp.float32).astype(jnp.bfloat16)
    grad_act = jnp.dot(cotangent, proj_out.T, preferred_element_type=jnp.float32)
    grad_pre = gelu_back(hidden_pre, grad_act).astype(jnp.bfloat16)
    grad_norm = jnp.dot(grad_pre, proj_in.T, preferred_element_type=jnp.float32)
    mean_grad = lax.optimization_barrier(jnp.mean(grad_norm, axis=1, keepdims=True))
    mean_cross = lax.optimization_barrier(jnp.mean(grad_norm * normed, axis=1, keepdims=True))
    patch_grad = (row_rstd * (grad_norm - mean_grad - normed * mean_cross)).astype(jnp.bfloat16)
    total_in = jnp.zeros((D, FF), jnp.float32)
    total_out = jnp.zeros((FF, D), jnp.float32)
    for block in range(N_DP):
        first = block * TOK_DEV
        rows_norm = normed_low[first:first + TOK_DEV]
        rows_pre = grad_pre[first:first + TOK_DEV]
        rows_act = activated[first:first + TOK_DEV]
        rows_cot = cotangent[first:first + TOK_DEV]
        total_in = total_in + rounded(jnp.dot(rows_norm.T, rows_pre, preferred_element_type=jnp.float32))
        total_out = total_out + rounded(jnp.dot(rows_act.T, rows_cot, preferred_element_type=jnp.float32))
    return (mlp_out, patch_grad, total_in.astype(jnp.bfloat16), total_out.astype(jnp.bfloat16))
```

```python
import jax
import jax.numpy as jnp
import numpy as np
from jax import lax
from jax.sharding import Mesh, PartitionSpec as P

eps = 1e-06
AXES = ("yh", "core", "yl", "x", "z")
SIZE = {"yh": 2, "core": 2, "yl": 2, "x": 4, "z": 8}
low = jnp.bfloat16
wide = jnp.float32


def shift(values, axis, step):
    count = SIZE[axis]
    return lax.ppermute(values, axis, [(i, (i + step) % count) for i in range(count)])


def put(buffer, piece, axis, at):
    return lax.dynamic_update_slice_in_dim(buffer, jnp.expand_dims(piece, axis), at, axis)


def take(buffer, axis, at):
    return lax.dynamic_index_in_dim(buffer, at, axis, keepdims=False)


def assemble(pieces, axis, me, count):
    first = pieces[0]
    shape = first.shape[:axis] + (count,) + first.shape[axis:]
    buffer = jnp.zeros(shape, first.dtype)
    for offset, piece in pieces.items():
        buffer = put(buffer, piece, axis, (me - offset) % count)
    return buffer


def ring_gather(block, axis):
    count = SIZE[axis]
    pieces = {0: block}
    up, down = block, block
    for step in range(1, count // 2):
        up, down = shift(up, axis, 1), shift(down, axis, -1)
        pieces[step], pieces[count - step] = up, down
    half = block.shape[-2] // 2
    far_up = shift(up[..., :half, :], axis, 1)
    far_down = shift(down[..., half:, :], axis, -1)
    pieces[count // 2] = jnp.concatenate([far_up, far_down], axis=-2)
    return pieces


def ring_scatter(chunk, axis):
    count = SIZE[axis]
    far = chunk(count // 2)
    half = far.shape[-2] // 2
    up = shift(far[..., :half, :].astype(low), axis, 1)
    down = shift(far[..., half:, :].astype(low), axis, -1)
    for step in range(count // 2 - 1, 0, -1):
        own_up, own_down = chunk(step), chunk(count - step)
        if step == count // 2 - 1:
            up = jnp.concatenate([own_up[..., :half, :] + up.astype(wide), own_up[..., half:, :]], axis=-2)
            down = jnp.concatenate([own_down[..., :half, :], own_down[..., half:, :] + down.astype(wide)], axis=-2)
        else:
            up, down = own_up + up.astype(wide), own_down + down.astype(wide)
        up, down = shift(up.astype(low), axis, 1), shift(down.astype(low), axis, -1)
    return chunk(0) + up.astype(wide) + down.astype(wide)


def direct_scatter(chunk, axis):
    count = SIZE[axis]
    total = chunk(0)
    for step in range(1, count):
        total = total + shift(chunk(step).astype(low), axis, step).astype(wide)
    return total


def per_device(patches, proj_in, proj_out, cotangent):
    tokens, own = patches.shape
    width = own * 64
    hidden = proj_in.shape[1]
    me = {axis: lax.axis_index(axis) for axis in AXES}

    both = jnp.concatenate([patches.T, cotangent.T], axis=0)
    other = shift(both, "yl", 1)
    pair = jnp.where(me["yl"] == 0, jnp.stack([both, other]), jnp.stack([other, both]))
    x_pair, c_pair = pair[:, :own], pair[:, own:]
    x_parts = {k: shift(x_pair, "z", k) if k else x_pair for k in range(8)}
    c_parts = {k: shift(c_pair, "x", k) if k else c_pair for k in range(4)}
    x_z = assemble(x_parts, 1, me["z"], 8)
    c_x = assemble(c_parts, 1, me["x"], 4)
    x_all = {k: shift(x_z, "x", k) if k else x_z for k in range(4)}
    c_all = ring_gather(c_x, "z")
    x_full = assemble(x_all, 1, me["x"], 4).reshape(width, tokens)
    cot = assemble(c_all, 2, me["z"], 8).reshape(width, tokens)

    wide_x = x_full.astype(wide)
    mean = jnp.sum(wide_x, axis=0, keepdims=True) / width
    var = jnp.sum(wide_x * wide_x, axis=0, keepdims=True) / width - mean * mean
    rstd = lax.rsqrt(var + eps)
    normed = (wide_x - mean) * rstd
    normed_low = normed.astype(low)

    def dot(first, second, one, two):
        return lax.dot_general(first, second, (((one,), (two,)), ((), ())), preferred_element_type=wide)

    hidden_pre = dot(proj_in, normed_low, 0, 0)
    grad_act = dot(proj_out, cot, 1, 0)
    act, back = jax.vjp(lambda values: jax.nn.gelu(values, approximate=True), hidden_pre)
    activated = act.astype(low)
    grad_pre = back(grad_act)[0].astype(low)

    share = dot(proj_out, activated, 0, 0).reshape(2, 4, 8, own, tokens)
    part = direct_scatter(lambda k: take(share, 1, (me["x"] + k) % 4), "x")
    part = direct_scatter(lambda k: take(part, 1, (me["z"] + k) % 8), "z")
    mlp_out = direct_scatter(lambda k: take(part, 0, (me["yl"] + k) % 2), "yl").astype(low).T

    share = dot(proj_in, grad_pre, 1, 0)
    mean_grad = jnp.sum(share, axis=0, keepdims=True) / width
    mean_cross = jnp.sum(share * normed, axis=0, keepdims=True) / width
    share = (rstd * (share - mean_grad - normed * mean_cross)).reshape(2, 4, 8, own, tokens)
    part = ring_scatter(lambda k: take(share, 2, (me["z"] + k) % 8), "z")
    part = direct_scatter(lambda k: take(part, 1, (me["x"] + k) % 4), "x")
    patch_grad = direct_scatter(lambda k: take(part, 0, (me["yl"] + k) % 2), "yl").astype(low).T

    quarter = width // 4

    def fold(value):
        kept = take(value, 1, me["core"]) + shift(take(value, 1, 1 - me["core"]), "core", 1).astype(wide)
        kept_low = kept.astype(low)
        away = take(kept_low, 0, 1 - me["yh"])
        half = away.shape[0] // 2
        got = jnp.concatenate([shift(away[:half], "yh", 1), shift(away[half:], "yh", 1)], axis=0)
        return (take(kept, 0, me["yh"]) + got.astype(wide)).astype(low)

    part_in = dot(normed_low, grad_pre, 1, 1).astype(low).reshape(2, 2, quarter, hidden)
    part_out = dot(activated, cot, 1, 1).astype(low).reshape(hidden, 2, 2, quarter).transpose(1, 2, 0, 3)
    total_in = fold(part_in)
    total_out = fold(part_out)
    return mlp_out, patch_grad, total_in, total_out


def solution(mesh):
    devices = np.asarray(mesh.devices).reshape([SIZE[axis] for axis in AXES])
    fine = Mesh(devices, AXES)
    dp, mp = ("yh", "core"), ("yl", "x", "z")
    in_specs = (P(dp, mp), P(None, mp), P(mp, None), P(dp, mp))
    out_specs = (P(dp, mp), P(dp, mp), P(dp, mp), P(mp, dp))
    return jax.shard_map(per_device, mesh=fine, in_specs=in_specs, out_specs=out_specs, check_vma=False)
```

```python
import functools
import math

import jax
import jax.numpy as jnp
import numpy as np
from jax import lax
from jax.experimental import pallas as pl
from jax.experimental.pallas import tpu as pltpu
from jax.sharding import Mesh, PartitionSpec as P

eps = 1e-06
AXES = ("yh", "core", "yl", "x", "z")
SIZE = {"yh": 2, "core": 2, "yl": 2, "x": 4, "z": 8}
low = jnp.bfloat16
wide = jnp.float32
TOK, OWN, HID, WIDTH = 256, 96, 384, 6144
HALF, BLOCK, QUARTER = WIDTH // 2, WIDTH // 8, WIDTH // 4
root = math.sqrt(2.0 / math.pi)


def shift(values, axis, step):
    count = SIZE[axis]
    return lax.ppermute(values, axis, [(i, (i + step) % count) for i in range(count)])


def kernel_call(body, outs, args, flops, scratch=()):
    def spec(value):
        if value.dtype == jnp.int32:
            return pl.BlockSpec(memory_space=pltpu.SMEM)
        return pl.BlockSpec(memory_space=pltpu.VMEM)

    shapes = [jax.ShapeDtypeStruct(shape, kind) for shape, kind in outs]
    moved = sum(math.prod(v.shape) * v.dtype.itemsize for v in [*args, *shapes])
    return pl.pallas_call(
        body,
        out_shape=shapes,
        in_specs=[spec(value) for value in args],
        out_specs=[pl.BlockSpec(memory_space=pltpu.VMEM) for _ in shapes],
        scratch_shapes=list(scratch),
        compiler_params=pltpu.CompilerParams(vmem_limit_bytes=40 << 20),
        cost_estimate=pl.CostEstimate(flops=flops, bytes_accessed=moved, transcendentals=0),
    )(*args)


def dot(first, second, one, two):
    return lax.dot_general(first, second, (((one,), (two,)), ((), ())), preferred_element_type=wide)


def block_start(yl, xi):
    return pl.multiple_of(yl * HALF + xi * BLOCK, BLOCK)


def hidden_body(me, p0, p1, p2, p3, mean, rstd, w, norm_ref, act_ref, act_t_ref, hid_t_ref, slope_t_ref, acc):
    acc[...] = jnp.zeros_like(acc)
    for k, piece in enumerate((p0, p1, p2, p3)):
        xi = (me[0] - k) & 3

        def step(yl, _, piece=piece, xi=xi):
            rows = pl.ds(block_start(yl, xi), BLOCK)
            value = ((piece[yl].astype(wide) - mean[...]) * rstd[...]).astype(low)
            norm_ref[rows, :] = value
            acc[...] += dot(value, w[rows, :], 0, 0)
            return 0

        lax.fori_loop(0, 2, step, 0)
    hidden = acc[...]
    square = hidden * hidden
    tanh = jnp.tanh(root * (hidden + 0.044715 * hidden * square))
    half = 0.5 * (1.0 + tanh)
    act = hidden * half
    slope = half + 0.5 * hidden * (1.0 - tanh * tanh) * (root * (1.0 + 3 * 0.044715 * square))
    act_ref[...] = act.astype(low)
    act_t_ref[...] = act.T.astype(low)
    hid_t_ref[...] = hidden.T
    slope_t_ref[...] = slope.T


def mlp_body(me, act, w, *outs):
    for k, out in enumerate(outs):
        xi = (me[0] + k) & 3

        def step(yl, _, out=out, xi=xi):
            out[yl] = dot(act[...], w[:, pl.ds(block_start(yl, xi), BLOCK)], 1, 0).astype(out.dtype)
            return 0

        lax.fori_loop(0, 2, step, 0)


def back_body(me, c0, c1, c2, c3, c5, c6, c7, far_up, far_down, w, slope_t, hid_t, col_sum, cot, grad_ref, grad_t_ref, means):
    def copy(piece, k, first, count):
        start = ((me[1] - k) & 7) * OWN + first

        def step(j, _):
            row = pl.multiple_of((j // 4) * HALF + (j % 4) * BLOCK + start, 16)
            cot[pl.ds(row, count), :] = piece[j // 4, j % 4]
            return 0

        lax.fori_loop(0, 8, step, 0)

    for k, piece in ((0, c0), (1, c1), (2, c2), (3, c3), (5, c5), (6, c6), (7, c7)):
        copy(piece, k, 0, OWN)
    copy(far_up, 4, 0, OWN // 2)
    copy(far_down, 4, OWN // 2, OWN // 2)
    grad_t = slope_t[...] * dot(w[...], cot[...], 1, 0)
    grad_low = grad_t.astype(low)
    grad_t_ref[...] = grad_low
    grad_ref[...] = grad_t.T.astype(low)
    rounded = grad_low.astype(wide)
    means[0:1, :] = jnp.sum(rounded * col_sum[...].T, axis=0, keepdims=True) / WIDTH
    means[1:2, :] = jnp.sum(rounded * hid_t[...], axis=0, keepdims=True) / WIDTH


def weight_in_body(me, norm, grad, mine, other, away):
    def part(yh, core):
        rows = pl.ds(pl.multiple_of((yh * 2 + core) * QUARTER, QUARTER), QUARTER)
        return dot(norm[rows, :], grad[...], 1, 0).astype(low)

    away[0] = part(me[3], 1 - me[4])
    away[1] = part(1 - me[3], 1 - me[4])
    other[...] = part(1 - me[3], me[4])
    mine[...] = part(me[3], me[4])


def weight_out_body(me, act_t, cot, mine, other, away):
    def part(yh, core):
        rows = pl.ds(pl.multiple_of((yh * 2 + core) * QUARTER, QUARTER), QUARTER)
        return dot(act_t[...], cot[rows, :], 1, 1).astype(low)

    away[0] = part(me[3], 1 - me[4])
    away[1] = part(1 - me[3], 1 - me[4])
    other[...] = part(1 - me[3], me[4])
    mine[...] = part(me[3], me[4])


def patch_body(me, p0, p1, p2, p3, mean, rstd, means, w, grad_t, *outs):
    pieces = (p0, p3, p2, p1)
    for k, out in enumerate(outs):
        xi = (me[0] + k) & 3

        def step(yl, _, out=out, xi=xi, piece=pieces[k]):
            share = dot(w[pl.ds(block_start(yl, xi), BLOCK), :], grad_t[...], 1, 0)
            normed = (piece[yl].astype(wide) - mean[...]) * rstd[...]
            share = rstd[...] * (share - means[0:1, :] - normed * means[1:2, :])
            out[yl] = share.astype(out.dtype)
            return 0

        lax.fori_loop(0, 2, step, 0)


def sum_body(turn, me, r0, r1, r2, r3, *outs_and_scratch):
    *outs, total = outs_and_scratch
    for yl in range(2):
        value = r0[yl].astype(wide) + r1[yl].astype(wide) + r2[yl].astype(wide) + r3[yl].astype(wide)
        total[yl] = value.T if turn else value
    for k, out in enumerate(outs):
        rows = pl.ds(pl.multiple_of(((me[1] + k) & 7) * OWN, 8), OWN)
        for yl in range(2):
            out[yl] = total[yl, rows, :].astype(out.dtype)


def gather_z(block, me):
    parts = [block] + [shift(block, "z", k) for k in range(1, 8)]
    buffer = jnp.zeros((2, 8, OWN, TOK), low)
    for k, part in enumerate(parts):
        buffer = lax.dynamic_update_slice_in_dim(buffer, part[:, None], (me - k) & 7, 1)
    return buffer.reshape(2, BLOCK, TOK)


def scatter(parts, turn, scalars, my_yl):
    got = [parts[0]] + [shift(parts[k], "x", k) for k in range(1, 4)]
    shapes = [((2, OWN, TOK), wide)] + [((2, OWN, TOK), low)] * 7
    blocks = kernel_call(
        functools.partial(sum_body, turn), shapes, [scalars, *got], 0, [pltpu.VMEM((2, BLOCK, TOK), wide)]
    )
    total = blocks[0]
    for k in range(1, 8):
        total = total + shift(blocks[k], "z", k).astype(wide)
    mine = jnp.where(my_yl == 0, total[0], total[1])
    other = jnp.where(my_yl == 0, total[1], total[0])
    return (mine + shift(other.astype(low), "yl", 1).astype(wide)).astype(low).T


def fold(parts):
    mine, other, away = parts
    got = shift(away, "core", 1)
    send = (other.astype(wide) + got[1].astype(wide)).astype(low)
    half = send.shape[0] // 2
    back = jnp.concatenate([shift(send[:half], "yh", 1), shift(send[half:], "yh", 1)], axis=0)
    return (mine.astype(wide) + got[0].astype(wide) + back.astype(wide)).astype(low)


def per_device(patches, proj_in, proj_out, cotangent):
    me = {axis: lax.axis_index(axis) for axis in AXES}
    scalars = jnp.stack([me["x"], me["z"], me["yl"], me["yh"], me["core"]]).astype(jnp.int32)
    work = 2 * TOK * WIDTH * HID

    both = jnp.concatenate([patches.T, cotangent.T], axis=0)
    near = shift(both, "yl", 1)
    pair = jnp.where(me["yl"] == 0, jnp.stack([both, near]), jnp.stack([near, both]))
    x_pair, c_pair = pair[:, :OWN], pair[:, OWN:]

    c_parts = [c_pair] + [shift(c_pair, "x", k) for k in range(1, 4)]
    c_x = jnp.zeros((2, 4, OWN, TOK), low)
    for k, part in enumerate(c_parts):
        c_x = lax.dynamic_update_slice_in_dim(c_x, part[:, None], (me["x"] - k) & 3, 1)
    x_z = gather_z(x_pair, me["z"])

    x_all = [x_z] + [shift(x_z, "x", k) for k in range(1, 4)]
    up, down = [c_x], [c_x]
    for _ in range(3):
        up.append(shift(up[-1], "z", 1))
        down.append(shift(down[-1], "z", -1))
    far_up = shift(up[3][:, :, : OWN // 2], "z", 1)
    far_down = shift(down[3][:, :, OWN // 2 :], "z", -1)

    total = sum(jnp.sum(part.astype(wide), axis=(0, 1)) for part in x_all)
    squares = sum(jnp.sum(part.astype(wide) * part.astype(wide), axis=(0, 1)) for part in x_all)
    mean = (total / WIDTH)[None]
    rstd = lax.rsqrt((squares / WIDTH)[None] - mean * mean + eps)
    col_sum = jnp.sum(proj_in.astype(wide), axis=0, keepdims=True)

    norm, act, act_t, hid_t, slope_t = kernel_call(
        hidden_body,
        [((WIDTH, TOK), low), ((TOK, HID), low), ((HID, TOK), low), ((HID, TOK), wide), ((HID, TOK), wide)],
        [scalars, *x_all, mean, rstd, proj_in],
        work,
        [pltpu.VMEM((TOK, HID), wide)],
    )
    mlp_parts = kernel_call(mlp_body, [((2, TOK, BLOCK), low)] * 4, [scalars, act, proj_out], work)
    cot, grad, grad_t, means = kernel_call(
        back_body,
        [((WIDTH, TOK), low), ((TOK, HID), low), ((HID, TOK), low), ((2, TOK), wide)],
        [scalars, *up, *down[:0:-1], far_up, far_down, proj_out, slope_t, hid_t, col_sum],
        work,
    )
    in_parts = kernel_call(
        weight_in_body, [((QUARTER, HID), low)] * 2 + [((2, QUARTER, HID), low)], [scalars, norm, grad], work
    )
    out_parts = kernel_call(
        weight_out_body, [((HID, QUARTER), low)] * 2 + [((2, HID, QUARTER), low)], [scalars, act_t, cot], work
    )
    patch_parts = kernel_call(
        patch_body,
        [((2, BLOCK, TOK), low)] * 4,
        [scalars, *x_all, mean, rstd, means, proj_in, grad_t],
        work,
    )
    mlp_out = scatter(mlp_parts, True, scalars, me["yl"])
    patch_grad = scatter(patch_parts, False, scalars, me["yl"])
    return mlp_out, patch_grad, fold(in_parts), fold(out_parts)


def solution(mesh):
    devices = np.asarray(mesh.devices).reshape([SIZE[axis] for axis in AXES])
    fine = Mesh(devices, AXES)
    dp, mp = ("yh", "core"), ("yl", "x", "z")
    in_specs = (P(dp, mp), P(None, mp), P(mp, None), P(dp, mp))
    out_specs = (P(dp, mp), P(dp, mp), P(dp, mp), P(mp, dp))
    return jax.shard_map(per_device, mesh=fine, in_specs=in_specs, out_specs=out_specs, check_vma=False)
```

```python
import math

import jax
import jax.numpy as jnp
import numpy as np
from jax import lax
from jax.experimental import pallas as pl
from jax.experimental.pallas import tpu as pltpu
from jax.sharding import Mesh, PartitionSpec as P

eps = 1e-06
AXES = ("yh", "core", "yl", "x", "z")
SIZE = {"yh": 2, "core": 2, "yl": 2, "x": 4, "z": 8}
low = jnp.bfloat16
wide = jnp.float32
TOK, OWN, HID, WIDTH = 256, 96, 384, 6144
HALF, BLOCK, QUARTER = WIDTH // 2, WIDTH // 8, WIDTH // 4
root = math.sqrt(2.0 / math.pi)
work = 2 * TOK * WIDTH * HID


def shift(values, axis, step):
    count = SIZE[axis]
    return lax.ppermute(values, axis, [(i, (i + step) % count) for i in range(count)])


def dot(first, second, one, two):
    return lax.dot_general(first, second, (((one,), (two,)), ((), ())), preferred_element_type=wide)


def whole(shape):
    return pl.BlockSpec(shape, lambda t, me: (0,) * len(shape))


def call(body, steps, scalars, ins, outs, scratch=(), after=(), flops=work):
    count = 1 + len(ins)

    def run(*refs):
        body(*refs[:count], *refs[count + len(after) :])

    shapes = [jax.ShapeDtypeStruct(shape, kind) for shape, kind, _ in outs]
    moved = sum(math.prod(v.shape) * v.dtype.itemsize for v in [*(a for a, _ in ins), *shapes])
    return pl.pallas_call(
        run,
        out_shape=shapes,
        grid_spec=pltpu.PrefetchScalarGridSpec(
            num_scalar_prefetch=1,
            grid=(steps,),
            in_specs=[spec for _, spec in ins] + [pl.BlockSpec(memory_space=pl.ANY) for _ in after],
            out_specs=[spec for _, _, spec in outs],
            scratch_shapes=list(scratch),
        ),
        compiler_params=pltpu.CompilerParams(vmem_limit_bytes=24 << 20),
        cost_estimate=pl.CostEstimate(flops=flops, bytes_accessed=moved, transcendentals=0),
    )(scalars, *(a for a, _ in ins), *after)


def block_at(me, k, yl):
    return yl * 4 + ((me[0] - k) & 3)


def rows_of(block):
    return pl.ds(pl.multiple_of(block * BLOCK, BLOCK), BLOCK)


def gelu_parts(hidden):
    square = hidden * hidden
    tanh = jnp.tanh(root * (hidden + 0.044715 * hidden * square))
    half = 0.5 * (1.0 + tanh)
    slope = half + 0.5 * hidden * (1.0 - tanh * tanh) * (root * (1.0 + 3 * 0.044715 * square))
    return hidden * half, slope


def main_body(me, p0, p1, p2, p3, mean, rstd, col_sum, w_in, w_out, part, *refs):
    mlp_outs, (patch, mine, other, away_mine, away_other) = refs[:4], refs[4:9]
    p_near, in_near, out_near, cot, norm, mlp_stage, patch_stage, grad_stage, acc, grad_acc = refs[9:19]
    p_sem, in_sem, out_sem, cot_sem, mlp_sem, patch_sem, grad_sem = refs[19:]

    def p_copy(t, piece, yl):
        return pltpu.make_async_copy(piece.at[yl], p_near.at[t], p_sem.at[t])

    def in_copy(t):
        return pltpu.make_async_copy(w_in.at[rows_of(block_at(me, t // 2, t % 2))], in_near.at[t], in_sem.at[t])

    def out_copy(j):
        return pltpu.make_async_copy(w_out.at[:, rows_of(j)], out_near.at[j], out_sem.at[j])

    def cot_copy(j):
        return pltpu.make_async_copy(part.at[:, (me[0] - (j % 4)) & 3, j // 4], cot.at[j], cot_sem.at[j])

    for t in range(8):
        p_copy(t, (p0, p1, p2, p3)[t // 2], t % 2).start()
        in_copy(t).start()
    for j in range(8):
        out_copy(j).start()
        cot_copy(j).start()
    acc[...] = jnp.zeros_like(acc)
    grad_acc[...] = jnp.zeros_like(grad_acc)

    def hidden_step(t, _):
        p_copy(t, p0, 0).wait()
        value = ((p_near[t].astype(wide) - mean[...]) * rstd[...]).astype(low)
        norm[block_at(me, t // 2, t % 2)] = value
        in_copy(t).wait()
        acc[...] += dot(value, in_near[t], 0, 0)
        return 0

    lax.fori_loop(0, 8, hidden_step, 0)

    def grad_step(j, _):
        out_copy(j).wait()
        cot_copy(j).wait()
        grad_acc[...] += dot(out_near[j], cot[j].reshape(BLOCK, TOK), 1, 0)
        return 0

    lax.fori_loop(0, 8, grad_step, 0)

    hidden = acc[...].T
    act_wide, slope = gelu_parts(hidden)
    act_t = act_wide.astype(low)
    act = act_wide.T.astype(low)
    grad_wide = slope * grad_acc[...]
    grad_t = grad_wide.astype(low)
    grad = grad_wide.T.astype(low)
    rounded = grad_t.astype(wide)
    first = jnp.sum(rounded * col_sum[...].T, axis=0, keepdims=True) / WIDTH
    second = jnp.sum(rounded * hidden, axis=0, keepdims=True) / WIDTH

    grad_to = (away_other, away_mine, other, mine)

    def grad_copy(q):
        return pltpu.make_async_copy(grad_stage.at[q], grad_to[q], grad_sem.at[q])

    for q in range(4):
        yh = me[3] if q in (1, 3) else 1 - me[3]
        core = 1 - me[4] if q < 2 else me[4]
        blocks = pl.ds((yh * 2 + core) * 2, 2)
        grad_stage[q, :QUARTER] = dot(norm[blocks].reshape(QUARTER, TOK), grad, 1, 0).astype(low)
        value = dot(act_t, cot[blocks].reshape(QUARTER, TOK), 1, 1).astype(low)
        for i in range(4):
            grad_stage[q, QUARTER + i * HID : QUARTER + (i + 1) * HID] = value[:, i * HID : (i + 1) * HID]
        grad_copy(q).start()

    def patch_copy(t):
        to = patch.at[:, t % 2, (me[0] - t // 2) & 3]
        return pltpu.make_async_copy(patch_stage.at[t], to, patch_sem.at[t])

    def patch_step(t, _):
        share = dot(in_near[t], grad_t, 1, 0)
        normed = (p_near[t].astype(wide) - mean[...]) * rstd[...]
        share = rstd[...] * (share - first - normed * second)
        patch_stage[t] = share.astype(low).reshape(8, OWN, TOK)
        patch_copy(t).start()
        return 0

    lax.fori_loop(0, 8, patch_step, 0)

    def mlp_copy(t):
        return pltpu.make_async_copy(mlp_stage.at[t], mlp_outs[t // 2].at[t % 2], mlp_sem.at[t])

    for t in range(8):
        mlp_stage[t] = dot(act, out_near[(t % 2) * 4 + ((me[0] + t // 2) & 3)], 1, 0).astype(low)
        mlp_copy(t).start()
    for t in range(8):
        patch_copy(t).wait()
        mlp_copy(t).wait()
    for q in range(4):
        grad_copy(q).wait()


def send_body(me, other, got, out):
    out[...] = (other[...].astype(wide) + got[...].astype(wide)).astype(low)


def final_body(me, mine, got, back, out):
    out[...] = (mine[...].astype(wide) + got[...].astype(wide) + back[...].astype(wide)).astype(low)


def sum_body(me, r0, r1, r2, r3, keep, away, total):
    value = r0[0].astype(wide) + r1[0].astype(wide) + r2[0].astype(wide) + r3[0].astype(wide)
    total[...] = value.T
    for d in range(4):
        pair = ((me[1] // 2 + d) & 3) * 2
        same = pl.ds(pl.multiple_of((pair + (me[1] & 1)) * OWN, 8), OWN)
        flip = pl.ds(pl.multiple_of((pair + 1 - (me[1] & 1)) * OWN, 8), OWN)
        keep[d, 0] = total[same, :]
        away[d, 0] = total[flip, :].astype(low)


def ring_z(block, near, me):
    up, down = near
    parts = {0: block, 1: up, 7: down}
    for step in (2, 3):
        up, down = shift(up, "z", 1), shift(down, "z", -1)
        parts[step], parts[8 - step] = up, down
    half = OWN // 2
    parts[4] = jnp.concatenate([shift(up[:, :half], "z", 1), shift(down[:, half:], "z", -1)], axis=1)
    buffer = jnp.zeros((2, 8, OWN, TOK), low)
    for k, part in parts.items():
        buffer = lax.dynamic_update_slice_in_dim(buffer, part[:, None], (me - k) & 7, 1)
    return buffer.reshape(2, BLOCK, TOK)


def last_step(total, my_yl):
    mine = jnp.where(my_yl == 0, total[0], total[1])
    other = jnp.where(my_yl == 0, total[1], total[0])
    return (mine + shift(other.astype(low), "yl", 1).astype(wide)).astype(low).T


def per_device(patches, proj_in, proj_out, cotangent):
    me = {axis: lax.axis_index(axis) for axis in AXES}
    scalars = jnp.stack([me["x"], me["z"], me["yl"], me["yh"], me["core"]]).astype(jnp.int32)

    both = jnp.concatenate([patches.T, cotangent.T], axis=0)
    near = shift(both, "yl", 1)
    pair = jnp.where(me["yl"] == 0, jnp.stack([both, near]), jnp.stack([near, both]))
    x_pair, c_pair = pair[:, :OWN], pair[:, OWN:]

    z_near = [shift(x_pair, "z", 1), shift(x_pair, "z", -1)]
    c_pair = jnp.where(me["z"] > 7, z_near[0], c_pair)
    c_parts = [c_pair] + [shift(c_pair, "x", k) for k in range(1, 4)]
    c_x = jnp.concatenate(c_parts, axis=0)
    c_all = lax.all_gather(c_x.reshape(8 * OWN, TOK), "z", axis=0, tiled=True).reshape(8, 4, 2, OWN, TOK)
    x_z = ring_z(x_pair, z_near, me["z"])
    x_all = [x_z] + [shift(x_z, "x", k) for k in range(1, 4)]

    total = sum(jnp.sum(part.astype(wide), axis=(0, 1)) for part in x_all)
    squares = sum(jnp.sum(part.astype(wide) * part.astype(wide), axis=(0, 1)) for part in x_all)
    mean = (total / WIDTH)[None]
    rstd = lax.rsqrt((squares / WIDTH)[None] - mean * mean + eps)
    col_sum = jnp.sum(proj_in.astype(wide), axis=0, keepdims=True)

    dma = pltpu.SemaphoreType.DMA
    near, far = pl.BlockSpec(memory_space=pltpu.VMEM), pl.BlockSpec(memory_space=pl.ANY)
    both_rows = 2 * QUARTER
    shapes = [(2, TOK, BLOCK)] * 4 + [(8, 2, 4, OWN, TOK), *[(both_rows, HID)] * 4]
    *mlp_parts, patch_parts, mine, other, away_mine, away_other = pl.pallas_call(
        main_body,
        out_shape=[jax.ShapeDtypeStruct(shape, low) for shape in shapes],
        in_specs=[pl.BlockSpec(memory_space=pltpu.SMEM)] + [far] * 4 + [near] * 3 + [far] * 3,
        out_specs=[far] * len(shapes),
        scratch_shapes=[
            pltpu.VMEM((8, BLOCK, TOK), low),
            pltpu.VMEM((8, BLOCK, HID), low),
            pltpu.VMEM((8, HID, BLOCK), low),
            pltpu.VMEM((8, 8, OWN, TOK), low),
            pltpu.VMEM((8, BLOCK, TOK), low),
            pltpu.VMEM((8, TOK, BLOCK), low),
            pltpu.VMEM((8, 8, OWN, TOK), low),
            pltpu.VMEM((4, both_rows, HID), low),
            pltpu.VMEM((TOK, HID), wide),
            pltpu.VMEM((HID, TOK), wide),
        ]
        + [dma((8,))] * 6
        + [dma((4,))],
        compiler_params=pltpu.CompilerParams(vmem_limit_bytes=60 << 20),
        cost_estimate=pl.CostEstimate(flops=6 * work, bytes_accessed=31 << 20, transcendentals=0),
    )(scalars, *x_all, mean, rstd, col_sum, proj_in, proj_out, c_all)

    got_other = shift(away_other, "core", 1)
    got_mine = shift(away_mine, "core", 1)
    backs, halves = [], []
    for half in range(2):
        rows = pl.BlockSpec((HID, HID), lambda t, me, half=half: (4 * half + t, 0))
        (send,) = call(
            send_body,
            4,
            scalars,
            [(other, rows), (got_other, rows)],
            [((QUARTER, HID), low, pl.BlockSpec((HID, HID), lambda t, me: (t, 0)))],
        )
        backs.append(shift(send, "yh", 1))
        halves.append(rows)

    mlp_got = [mlp_parts[0]] + [shift(mlp_parts[k], "x", k) for k in range(1, 4)]
    keep, flip = call(
        sum_body,
        2,
        scalars,
        [(part, pl.BlockSpec((1, TOK, BLOCK), lambda t, me: (t, 0, 0))) for part in mlp_got],
        [((4, 2, OWN, TOK), kind, pl.BlockSpec((4, 1, OWN, TOK), lambda t, me: (0, t, 0, 0))) for kind in (wide, low)],
        [pltpu.VMEM((BLOCK, TOK), wide)],
        after=[backs[0]],
    )
    keep = keep + lax.ppermute(flip, "z", [(i, i ^ 1) for i in range(8)]).astype(wide)
    total = keep[0]
    for d in range(1, 4):
        total = total + shift(keep[d].astype(low), "z", 2 * d).astype(wide)
    mlp_out = last_step(total, me["yl"])

    part = lax.psum_scatter(patch_parts.reshape(WIDTH, TOK), "z", scatter_dimension=0, tiled=True)
    part = part.reshape(2, 4, OWN, TOK)
    total = lax.dynamic_index_in_dim(part, me["x"], 1, keepdims=False).astype(wide)
    for k in range(1, 4):
        away = lax.dynamic_index_in_dim(part, (me["x"] + k) & 3, 1, keepdims=False)
        total = total + shift(away, "x", k).astype(wide)
    patch_grad = last_step(total, me["yl"])

    own_rows = pl.BlockSpec((HID, HID), lambda t, me: (t, 0))
    own_cols = pl.BlockSpec((HID, HID), lambda t, me: (0, t))
    grad_in, grad_out = (
        call(
            final_body,
            4,
            scalars,
            [(mine, rows), (got_mine, rows), (back, own_rows)],
            [(shape, low, to)],
        )[0]
        for rows, back, shape, to in (
            (halves[0], backs[0], (QUARTER, HID), own_rows),
            (halves[1], backs[1], (HID, QUARTER), own_cols),
        )
    )
    return mlp_out, patch_grad, grad_in, grad_out


def solution(mesh):
    devices = np.asarray(mesh.devices).reshape([SIZE[axis] for axis in AXES])
    fine = Mesh(devices, AXES)
    dp, mp = ("yh", "core"), ("yl", "x", "z")
    in_specs = (P(dp, mp), P(None, mp), P(mp, None), P(dp, mp))
    out_specs = (P(dp, mp), P(dp, mp), P(dp, mp), P(mp, dp))
    return jax.shard_map(per_device, mesh=fine, in_specs=in_specs, out_specs=out_specs, check_vma=False)
```

```python
import functools
import math

import jax
import jax.numpy as jnp
import numpy as np
from jax import lax
from jax.experimental import pallas as pl
from jax.experimental.pallas import tpu as pltpu
from jax.sharding import Mesh, PartitionSpec as P

eps = 1e-06
AXES = ("yh", "core", "yl", "x", "z")
SIZE = {"yh": 2, "core": 2, "yl": 2, "x": 4, "z": 8}
low = jnp.bfloat16
wide = jnp.float32
TOK, OWN, HID, WIDTH = 256, 96, 384, 6144
HALF, BLOCK, QUARTER = WIDTH // 2, WIDTH // 8, WIDTH // 4
NEAR = 80
REST = OWN - NEAR
FAR = OWN + REST
root = math.sqrt(2.0 / math.pi)
work = 2 * TOK * WIDTH * HID


def shift(values, axis, step):
    count = SIZE[axis]
    return lax.ppermute(values, axis, [(i, (i + step) % count) for i in range(count)])


def dot(first, second, one, two):
    return lax.dot_general(first, second, (((one,), (two,)), ((), ())), preferred_element_type=wide)


def whole(shape):
    return pl.BlockSpec(shape, lambda t, me: (0,) * len(shape))


def call(body, steps, scalars, ins, outs, scratch=(), after=(), flops=work):
    count = 1 + len(ins)

    def run(*refs):
        body(*refs[:count], *refs[count + len(after) :])

    shapes = [jax.ShapeDtypeStruct(shape, kind) for shape, kind, _ in outs]
    moved = sum(math.prod(v.shape) * v.dtype.itemsize for v in [*(a for a, _ in ins), *shapes])
    return pl.pallas_call(
        run,
        out_shape=shapes,
        grid_spec=pltpu.PrefetchScalarGridSpec(
            num_scalar_prefetch=1,
            grid=(steps,),
            in_specs=[spec for _, spec in ins] + [pl.BlockSpec(memory_space=pl.ANY) for _ in after],
            out_specs=[spec for _, _, spec in outs],
            scratch_shapes=list(scratch),
        ),
        compiler_params=pltpu.CompilerParams(vmem_limit_bytes=24 << 20),
        cost_estimate=pl.CostEstimate(flops=flops, bytes_accessed=moved, transcendentals=0),
    )(scalars, *(a for a, _ in ins), *after)


def block_at(me, k, yl):
    return yl * 4 + ((me[0] - k) & 3)


def rows_of(block):
    return pl.ds(pl.multiple_of(block * BLOCK, BLOCK), BLOCK)


def gelu_parts(hidden):
    square = hidden * hidden
    tanh = jnp.tanh(root * (hidden + 0.044715 * hidden * square))
    half = 0.5 * (1.0 + tanh)
    slope = half + 0.5 * hidden * (1.0 - tanh * tanh) * (root * (1.0 + 3 * 0.044715 * square))
    return hidden * half, slope


def main_body(me, p0, p1, p2, p3, col_sum, w_in, w_out, part, *refs):
    mlp_outs, (patch, mine, other, away_mine, away_other) = refs[:4], refs[4:9]
    p_near, in_near, out_near, cot, norm, mlp_stage, rest_stage, patch_stage, grad_stage, acc, grad_acc = refs[9:20]
    p_sem, rest_sem, in_sem, out_sem, cot_sem, mlp_sem, mlp_rest_sem, patch_sem, grad_sem = refs[20:]
    first_rows, rest_rows, far_rows = pl.ds(0, NEAR), pl.ds(NEAR, REST), pl.ds(OWN, REST)

    def p_copy(t, piece, yl):
        return pltpu.make_async_copy(piece.at[yl], p_near.at[t, :, first_rows], p_sem.at[t])

    def rest_copy(t):
        source = part.at[:, t // 2, t % 2, far_rows]
        return pltpu.make_async_copy(source, p_near.at[t, :, rest_rows], rest_sem.at[t])

    def in_copy(t):
        return pltpu.make_async_copy(w_in.at[rows_of(block_at(me, t // 2, t % 2))], in_near.at[t], in_sem.at[t])

    def out_copy(j):
        return pltpu.make_async_copy(w_out.at[:, rows_of(j)], out_near.at[j], out_sem.at[j])

    def cot_copy(j):
        source = part.at[:, (me[0] - (j % 4)) & 3, j // 4, pl.ds(0, OWN)]
        return pltpu.make_async_copy(source, cot.at[j], cot_sem.at[j])

    for t in range(8):
        p_copy(t, (p0, p1, p2, p3)[t // 2], t % 2).start()
        rest_copy(t).start()
    for t in range(8):
        in_copy(t).start()
    for j in range(8):
        out_copy(j).start()
        cot_copy(j).start()
    acc[...] = jnp.zeros_like(acc)
    grad_acc[...] = jnp.zeros_like(grad_acc)

    def sums_step(t, sums):
        p_copy(t, p0, 0).wait()
        rest_copy(t).wait()
        value = p_near[t].reshape(BLOCK, TOK).astype(wide)
        return sums[0] + jnp.sum(value, axis=0, keepdims=True), sums[1] + jnp.sum(value * value, axis=0, keepdims=True)

    zero = jnp.zeros((1, TOK), wide)
    sums = lax.fori_loop(0, 8, sums_step, (zero, zero))
    mean = sums[0] / WIDTH
    rstd = lax.rsqrt(sums[1] / WIDTH - mean * mean + eps)

    def hidden_step(t, _):
        value = ((p_near[t].reshape(BLOCK, TOK).astype(wide) - mean) * rstd).astype(low)
        norm[block_at(me, t // 2, t % 2)] = value
        in_copy(t).wait()
        acc[...] += dot(value, in_near[t], 0, 0)
        return 0

    lax.fori_loop(0, 8, hidden_step, 0)

    def grad_step(j, _):
        out_copy(j).wait()
        cot_copy(j).wait()
        grad_acc[...] += dot(out_near[j], cot[j].reshape(BLOCK, TOK), 1, 0)
        return 0

    lax.fori_loop(0, 8, grad_step, 0)

    hidden = acc[...].T
    act_wide, slope = gelu_parts(hidden)
    act_t = act_wide.astype(low)
    act = act_wide.T.astype(low)
    grad_wide = slope * grad_acc[...]
    grad_t = grad_wide.astype(low)
    grad = grad_wide.T.astype(low)
    rounded = grad_t.astype(wide)
    first = jnp.sum(rounded * col_sum[...].T, axis=0, keepdims=True) / WIDTH
    second = jnp.sum(rounded * hidden, axis=0, keepdims=True) / WIDTH

    grad_to = (away_other, away_mine, other, mine)

    def grad_copy(q):
        return pltpu.make_async_copy(grad_stage.at[q], grad_to[q], grad_sem.at[q])

    for q in range(4):
        yh = me[3] if q in (1, 3) else 1 - me[3]
        core = 1 - me[4] if q < 2 else me[4]
        blocks = pl.ds((yh * 2 + core) * 2, 2)
        grad_stage[q, :QUARTER] = dot(norm[blocks].reshape(QUARTER, TOK), grad, 1, 0).astype(low)
        value = dot(act_t, cot[blocks].reshape(QUARTER, TOK), 1, 1).astype(low)
        for i in range(4):
            grad_stage[q, QUARTER + i * HID : QUARTER + (i + 1) * HID] = value[:, i * HID : (i + 1) * HID]
        grad_copy(q).start()

    def patch_copy(t):
        to = patch.at[:, t % 2, (me[0] - t // 2) & 3, pl.ds(0, OWN)]
        return pltpu.make_async_copy(patch_stage.at[t], to, patch_sem.at[t])

    def patch_step(t, _):
        share = dot(in_near[t], grad_t, 1, 0)
        normed = (p_near[t].reshape(BLOCK, TOK).astype(wide) - mean) * rstd
        share = rstd * (share - first - normed * second)
        patch_stage[t] = share.astype(low).reshape(8, OWN, TOK)
        patch_copy(t).start()
        return 0

    lax.fori_loop(0, 8, patch_step, 0)

    def mlp_copy(t):
        return pltpu.make_async_copy(mlp_stage.at[t], mlp_outs[t // 2].at[t % 2], mlp_sem.at[t])

    def mlp_rest_copy(t):
        to = patch.at[:, t % 2, (me[0] + t // 2) & 3, far_rows]
        return pltpu.make_async_copy(rest_stage.at[t], to, mlp_rest_sem.at[t])

    for t in range(8):
        value = dot(act, out_near[(t % 2) * 4 + ((me[0] + t // 2) & 3)], 1, 0)
        value = value.T.astype(low).reshape(8, OWN, TOK)
        mlp_stage[t] = value[:, :NEAR]
        mlp_copy(t).start()
        rest_stage[t] = value[:, NEAR:]
        mlp_rest_copy(t).start()
    for t in range(8):
        patch_copy(t).wait()
        mlp_copy(t).wait()
        mlp_rest_copy(t).wait()
    for q in range(4):
        grad_copy(q).wait()


def add_body(count, plan, me, *refs):
    ins, rest = refs[:count], refs[count:]
    into, stage, in_sem, out_sem = rest[-4:]

    def fetch(i):
        return [
            pltpu.make_async_copy(ins[which].at[pl.ds(row, HID)], into.at[i, n], in_sem.at[i, n])
            for n, (which, row) in enumerate(plan[i][0])
        ]

    def store(i):
        which, at, across = plan[i][1]
        block = pl.ds(at, HID)
        return pltpu.make_async_copy(stage.at[i], rest[which].at[:, block] if across else rest[which].at[block], out_sem.at[i])

    for i in range(len(plan)):
        for copy in fetch(i):
            copy.start()
    for i in range(len(plan)):
        for copy in fetch(i):
            copy.wait()
        stage[i] = sum(into[i, n].astype(wide) for n in range(len(plan[i][0]))).astype(low)
        store(i).start()
    for i in range(len(plan)):
        store(i).wait()


def add_call(scalars, arrays, shapes, plan):
    far = pl.BlockSpec(memory_space=pl.ANY)
    blocks, terms = len(plan), len(plan[0][0])
    dma = pltpu.SemaphoreType.DMA
    return pl.pallas_call(
        functools.partial(add_body, len(arrays), plan),
        out_shape=[jax.ShapeDtypeStruct(shape, low) for shape in shapes],
        in_specs=[pl.BlockSpec(memory_space=pltpu.SMEM)] + [far] * len(arrays),
        out_specs=[far] * len(shapes),
        scratch_shapes=[
            pltpu.VMEM((blocks, terms, HID, HID), low),
            pltpu.VMEM((blocks, HID, HID), low),
            dma((blocks, terms)),
            dma((blocks,)),
        ],
        compiler_params=pltpu.CompilerParams(vmem_limit_bytes=60 << 20),
        cost_estimate=pl.CostEstimate(flops=0, bytes_accessed=0, transcendentals=0),
    )(scalars, *arrays)


def sum_body(me, r0, r1, r2, r3, keep, away, total):
    total[...] = r0[0].astype(wide) + r1[0].astype(wide) + r2[0].astype(wide) + r3[0].astype(wide)
    for d in range(4):
        pair = ((me[1] // 2 + d) & 3) * 2
        keep[d, 0] = total[pair + (me[1] & 1)]
        away[d, 0] = total[pair + 1 - (me[1] & 1)].astype(low)


def ring_z(block, me):
    up = down = block
    parts = {0: block}
    for step in (1, 2, 3):
        up, down = shift(up, "z", 1), shift(down, "z", -1)
        parts[step], parts[8 - step] = up, down
    half = NEAR // 2 // 16 * 16
    parts[4] = jnp.concatenate([shift(up[:, :half], "z", 1), shift(down[:, half:], "z", -1)], axis=1)
    buffer = jnp.zeros((2, 8, *block.shape[1:]), low)
    for k, part in parts.items():
        buffer = lax.dynamic_update_slice_in_dim(buffer, part[:, None], (me - k) & 7, 1)
    return buffer


def per_device(patches, proj_in, proj_out, cotangent):
    me = {axis: lax.axis_index(axis) for axis in AXES}
    scalars = jnp.stack([me["x"], me["z"], me["yl"], me["yh"], me["core"]]).astype(jnp.int32)

    both = jnp.concatenate([patches.T, cotangent.T], axis=0)
    near = shift(both, "yl", 1)
    pair = jnp.where(me["yl"] == 0, jnp.stack([both, near]), jnp.stack([near, both]))
    x_pair, c_pair = pair[:, :OWN], pair[:, OWN:]

    c_pair = jnp.concatenate([c_pair, x_pair[:, NEAR:]], axis=1)
    c_parts = [c_pair] + [shift(c_pair, "x", k) for k in range(1, 4)]
    c_x = jnp.concatenate(c_parts, axis=0)
    c_all = lax.all_gather(c_x.reshape(8 * FAR, TOK), "z", axis=0, tiled=True).reshape(8, 4, 2, FAR, TOK)
    x_z = ring_z(x_pair[:, :NEAR], me["z"])
    x_all = [x_z] + [shift(x_z, "x", k) for k in range(1, 4)]

    col_sum = jnp.sum(proj_in.astype(wide), axis=0, keepdims=True)

    dma = pltpu.SemaphoreType.DMA
    near, far = pl.BlockSpec(memory_space=pltpu.VMEM), pl.BlockSpec(memory_space=pl.ANY)
    both_rows = 2 * QUARTER
    shapes = [(2, 8, NEAR, TOK)] * 4 + [(8, 2, 4, FAR, TOK)] + [(both_rows, HID)] * 4
    params = pltpu.CompilerParams(vmem_limit_bytes=60 << 20)
    *mlp_parts, patch_parts, mine, other, away_mine, away_other = pl.pallas_call(
        main_body,
        out_shape=[jax.ShapeDtypeStruct(shape, low) for shape in shapes],
        in_specs=[pl.BlockSpec(memory_space=pltpu.SMEM)] + [far] * 4 + [near] + [far] * 3,
        out_specs=[far] * len(shapes),
        scratch_shapes=[
            pltpu.VMEM((8, 8, OWN, TOK), low),
            pltpu.VMEM((8, BLOCK, HID), low),
            pltpu.VMEM((8, HID, BLOCK), low),
            pltpu.VMEM((8, 8, OWN, TOK), low),
            pltpu.VMEM((8, BLOCK, TOK), low),
            pltpu.VMEM((8, 8, NEAR, TOK), low),
            pltpu.VMEM((8, 8, REST, TOK), low),
            pltpu.VMEM((8, 8, OWN, TOK), low),
            pltpu.VMEM((4, both_rows, HID), low),
            pltpu.VMEM((TOK, HID), wide),
            pltpu.VMEM((HID, TOK), wide),
        ]
        + [dma((8,))] * 8
        + [dma((4,))],
        compiler_params=params,
        cost_estimate=pl.CostEstimate(flops=6 * work, bytes_accessed=31 << 20, transcendentals=0),
    )(scalars, *x_all, col_sum, proj_in, proj_out, c_all)

    got_other = shift(away_other, "core", 1)
    got_mine = shift(away_mine, "core", 1)


    starts = range(0, both_rows, HID)
    backs = []
    for some in (starts[:2], starts[2:]):
        plan = [([(0, row), (1, row)], (0, row - some[0], False)) for row in some]
        (send,) = add_call(scalars, [other, got_other], [(len(some) * HID, HID)], plan)
        backs.append(shift(send, "yh", 1))

    mlp_got = [mlp_parts[0]] + [shift(mlp_parts[k], "x", k) for k in range(1, 4)]
    keep, flip = call(
        sum_body,
        2,
        scalars,
        [(part, pl.BlockSpec((1, 8, NEAR, TOK), lambda t, me: (t, 0, 0, 0))) for part in mlp_got],
        [((4, 2, NEAR, TOK), kind, pl.BlockSpec((4, 1, NEAR, TOK), lambda t, me: (0, t, 0, 0))) for kind in (wide, low)],
        [pltpu.VMEM((8, NEAR, TOK), wide)],
        after=[got_mine, backs[0]],
    )
    keep = keep + lax.ppermute(flip, "z", [(i, i ^ 1) for i in range(8)]).astype(wide)
    total = keep[0]
    for d in range(1, 4):
        total = total + shift(keep[d].astype(low), "z", 2 * d).astype(wide)

    rest = lax.psum_scatter(patch_parts.reshape(64 * FAR, TOK), "z", scatter_dimension=0, tiled=True)
    rest = rest.reshape(2, 4, FAR, TOK)
    rest_total = lax.dynamic_index_in_dim(rest, me["x"], 1, keepdims=False).astype(wide)
    for k in range(1, 4):
        block = lax.dynamic_index_in_dim(rest, (me["x"] + k) & 3, 1, keepdims=False)
        rest_total = rest_total + shift(block, "x", k).astype(wide)

    total = jnp.concatenate([rest_total, total], axis=1)
    mine_y = jnp.where(me["yl"] == 0, total[0], total[1])
    other_y = jnp.where(me["yl"] == 0, total[1], total[0])
    result = (mine_y + shift(other_y.astype(low), "yl", 1).astype(wide)).astype(low)
    patch_grad = result[:OWN].T
    mlp_out = jnp.concatenate([result[FAR:], result[OWN:FAR]], axis=0).T

    plan = []
    for i, row in enumerate(starts):
        back = (2, row) if i < 2 else (3, row - starts[2])
        plan.append(([(0, row), (1, row), back], (i // 4, i % 4 * HID, i > 3)))
    grad_in, grad_out = add_call(scalars, [mine, got_mine, *backs], [(QUARTER, HID), (HID, QUARTER)], plan)
    return mlp_out, patch_grad, grad_in, grad_out


def solution(mesh):
    devices = np.asarray(mesh.devices).reshape([SIZE[axis] for axis in AXES])
    fine = Mesh(devices, AXES)
    dp, mp = ("yh", "core"), ("yl", "x", "z")
    in_specs = (P(dp, mp), P(None, mp), P(mp, None), P(dp, mp))
    out_specs = (P(dp, mp), P(dp, mp), P(dp, mp), P(mp, dp))
    return jax.shard_map(per_device, mesh=fine, in_specs=in_specs, out_specs=out_specs, check_vma=False)
```

```python
import functools
import math

import jax
import jax.numpy as jnp
import numpy as np
from jax import lax
from jax.experimental import pallas as pl
from jax.experimental.pallas import tpu as pltpu
from jax.sharding import Mesh, PartitionSpec as P

eps = 1e-06
AXES = ("yh", "core", "yl", "x", "z")
SIZE = {"yh": 2, "core": 2, "yl": 2, "x": 4, "z": 8}
low = jnp.bfloat16
wide = jnp.float32
TOK, OWN, HID, WIDTH = 256, 96, 384, 6144
HALF, BLOCK, QUARTER = WIDTH // 2, WIDTH // 8, WIDTH // 4
NEAR = 80
REST = OWN - NEAR
FAR = OWN + REST
root = math.sqrt(2.0 / math.pi)
work = 2 * TOK * WIDTH * HID


def shift(values, axis, step):
    count = SIZE[axis]
    return lax.ppermute(values, axis, [(i, (i + step) % count) for i in range(count)])


def dot(first, second, one, two):
    return lax.dot_general(first, second, (((one,), (two,)), ((), ())), preferred_element_type=wide)


def whole(shape):
    return pl.BlockSpec(shape, lambda t, me: (0,) * len(shape))


def call(body, steps, scalars, ins, outs, scratch=(), after=(), flops=work):
    count = 1 + len(ins)

    def run(*refs):
        body(*refs[:count], *refs[count + len(after) :])

    shapes = [jax.ShapeDtypeStruct(shape, kind) for shape, kind, _ in outs]
    moved = sum(math.prod(v.shape) * v.dtype.itemsize for v in [*(a for a, _ in ins), *shapes])
    return pl.pallas_call(
        run,
        out_shape=shapes,
        grid_spec=pltpu.PrefetchScalarGridSpec(
            num_scalar_prefetch=1,
            grid=(steps,),
            in_specs=[spec for _, spec in ins] + [pl.BlockSpec(memory_space=pl.ANY) for _ in after],
            out_specs=[spec for _, _, spec in outs],
            scratch_shapes=list(scratch),
        ),
        compiler_params=pltpu.CompilerParams(vmem_limit_bytes=24 << 20),
        cost_estimate=pl.CostEstimate(flops=flops, bytes_accessed=moved, transcendentals=0),
    )(scalars, *(a for a, _ in ins), *after)


def block_at(me, k, yl):
    return yl * 4 + ((me[0] - k) & 3)


def rows_of(block):
    return pl.ds(pl.multiple_of(block * BLOCK, BLOCK), BLOCK)


def gelu_parts(hidden):
    square = hidden * hidden
    tanh = jnp.tanh(root * (hidden + 0.044715 * hidden * square))
    half = 0.5 * (1.0 + tanh)
    slope = half + 0.5 * hidden * (1.0 - tanh * tanh) * (root * (1.0 + 3 * 0.044715 * square))
    return hidden * half, slope


def main_body(me, p0, p1, p2, p3, col_sum, w_in, w_out, part, *refs):
    mlp_outs, (patch, norm_out, act_out, grad_out) = refs[:4], refs[4:8]
    p_near, in_near, out_near, cot, norm, mlp_stage, rest_stage, patch_stage, act_near, grad_near, acc, grad_acc = refs[8:20]
    p_sem, rest_sem, in_sem, out_sem, cot_sem, mlp_sem, mlp_rest_sem, patch_sem, extra_sem = refs[20:]
    first_rows, rest_rows, far_rows = pl.ds(0, NEAR), pl.ds(NEAR, REST), pl.ds(OWN, REST)

    def p_copy(t, piece, yl):
        return pltpu.make_async_copy(piece.at[yl], p_near.at[t, :, first_rows], p_sem.at[t])

    def rest_copy(t):
        source = part.at[:, t // 2, t % 2, far_rows]
        return pltpu.make_async_copy(source, p_near.at[t, :, rest_rows], rest_sem.at[t])

    def in_copy(t):
        return pltpu.make_async_copy(w_in.at[rows_of(block_at(me, t // 2, t % 2))], in_near.at[t], in_sem.at[t])

    def out_copy(j):
        return pltpu.make_async_copy(w_out.at[:, rows_of(j)], out_near.at[j], out_sem.at[j])

    def cot_copy(j):
        source = part.at[:, (me[0] - (j % 4)) & 3, j // 4, pl.ds(0, OWN)]
        return pltpu.make_async_copy(source, cot.at[j], cot_sem.at[j])

    for t in range(8):
        p_copy(t, (p0, p1, p2, p3)[t // 2], t % 2).start()
        rest_copy(t).start()
    for t in range(8):
        in_copy(t).start()
    for j in range(8):
        out_copy(j).start()
        cot_copy(j).start()
    acc[...] = jnp.zeros_like(acc)
    grad_acc[...] = jnp.zeros_like(grad_acc)

    def sums_step(t, sums):
        p_copy(t, p0, 0).wait()
        rest_copy(t).wait()
        value = p_near[t].reshape(BLOCK, TOK).astype(wide)
        return sums[0] + jnp.sum(value, axis=0, keepdims=True), sums[1] + jnp.sum(value * value, axis=0, keepdims=True)

    zero = jnp.zeros((1, TOK), wide)
    sums = lax.fori_loop(0, 8, sums_step, (zero, zero))
    mean = sums[0] / WIDTH
    rstd = lax.rsqrt(sums[1] / WIDTH - mean * mean + eps)

    def hidden_step(t, _):
        value = ((p_near[t].reshape(BLOCK, TOK).astype(wide) - mean) * rstd).astype(low)
        norm[block_at(me, t // 2, t % 2)] = value
        in_copy(t).wait()
        acc[...] += dot(value, in_near[t], 0, 0)
        return 0

    lax.fori_loop(0, 8, hidden_step, 0)

    def grad_step(j, _):
        out_copy(j).wait()
        cot_copy(j).wait()
        grad_acc[...] += dot(out_near[j], cot[j].reshape(BLOCK, TOK), 1, 0)
        return 0

    lax.fori_loop(0, 8, grad_step, 0)

    hidden = acc[...].T
    act_wide, slope = gelu_parts(hidden)
    act_t = act_wide.astype(low)
    act = act_wide.T.astype(low)
    grad_wide = slope * grad_acc[...]
    grad_t = grad_wide.astype(low)
    grad = grad_wide.T.astype(low)
    rounded = grad_t.astype(wide)
    first = jnp.sum(rounded * col_sum[...].T, axis=0, keepdims=True) / WIDTH
    second = jnp.sum(rounded * hidden, axis=0, keepdims=True) / WIDTH

    act_near[...] = act_t
    grad_near[...] = grad
    extra = [
        pltpu.make_async_copy(source, to, extra_sem.at[i])
        for i, (source, to) in enumerate(((norm, norm_out), (act_near, act_out), (grad_near, grad_out)))
    ]
    for copy in extra:
        copy.start()

    def patch_copy(t):
        to = patch.at[:, t % 2, (me[0] - t // 2) & 3, pl.ds(0, OWN)]
        return pltpu.make_async_copy(patch_stage.at[t], to, patch_sem.at[t])

    def patch_step(t, _):
        share = dot(in_near[t], grad_t, 1, 0)
        normed = (p_near[t].reshape(BLOCK, TOK).astype(wide) - mean) * rstd
        share = rstd * (share - first - normed * second)
        patch_stage[t] = share.astype(low).reshape(8, OWN, TOK)
        patch_copy(t).start()
        return 0

    lax.fori_loop(0, 8, patch_step, 0)

    def mlp_copy(t):
        return pltpu.make_async_copy(mlp_stage.at[t], mlp_outs[t // 2].at[t % 2], mlp_sem.at[t])

    def mlp_rest_copy(t):
        to = patch.at[:, t % 2, (me[0] + t // 2) & 3, far_rows]
        return pltpu.make_async_copy(rest_stage.at[t], to, mlp_rest_sem.at[t])

    for t in range(8):
        value = dot(act, out_near[(t % 2) * 4 + ((me[0] + t // 2) & 3)], 1, 0)
        value = value.T.astype(low).reshape(8, OWN, TOK)
        mlp_stage[t] = value[:, :NEAR]
        mlp_copy(t).start()
        rest_stage[t] = value[:, NEAR:]
        mlp_rest_copy(t).start()
    for t in range(8):
        patch_copy(t).wait()
        mlp_copy(t).wait()
        mlp_rest_copy(t).wait()
    for copy in extra:
        copy.wait()


def weights_body(me, part, norm_in, act_in, grad_in, mine, other, away_mine, away_other, *refs):
    cot, norm, act_near, grad_near, grad_stage, cot_sem, norm_sem, small_sem, grad_sem = refs

    def spot(q):
        yh = me[3] if q in (1, 3) else 1 - me[3]
        return (yh * 2 + (1 - me[4] if q < 2 else me[4])) * 2

    def cot_copy(q, i):
        j = spot(q) + i
        source = part.at[:, (me[0] - (j % 4)) & 3, j // 4, pl.ds(0, OWN)]
        return pltpu.make_async_copy(source, cot.at[2 * q + i], cot_sem.at[2 * q + i])

    def norm_copy(q):
        return pltpu.make_async_copy(norm_in.at[pl.ds(spot(q), 2)], norm.at[q], norm_sem.at[q])

    small = [
        pltpu.make_async_copy(grad_in, grad_near, small_sem.at[0]),
        pltpu.make_async_copy(act_in, act_near, small_sem.at[1]),
    ]
    for copy in small:
        copy.start()
    for q in range(4):
        norm_copy(q).start()
        cot_copy(q, 0).start()
        cot_copy(q, 1).start()
    for copy in small:
        copy.wait()
    grad, act_t = grad_near[...], act_near[...]

    grad_to = (away_other, away_mine, other, mine)

    def grad_copy(q):
        return pltpu.make_async_copy(grad_stage.at[q], grad_to[q], grad_sem.at[q])

    for q in range(4):
        norm_copy(q).wait()
        grad_stage[q, :QUARTER] = dot(norm[q].reshape(QUARTER, TOK), grad, 1, 0).astype(low)
        cot_copy(q, 0).wait()
        cot_copy(q, 1).wait()
        value = dot(act_t, cot[2 * q : 2 * q + 2].reshape(QUARTER, TOK), 1, 1).astype(low)
        for i in range(4):
            grad_stage[q, QUARTER + i * HID : QUARTER + (i + 1) * HID] = value[:, i * HID : (i + 1) * HID]
        grad_copy(q).start()
    for q in range(4):
        grad_copy(q).wait()


def add_body(count, plan, me, *refs):
    ins, rest = refs[:count], refs[count:]
    into, stage, in_sem, out_sem = rest[-4:]

    def fetch(i):
        return [
            pltpu.make_async_copy(ins[which].at[pl.ds(row, HID)], into.at[i, n], in_sem.at[i, n])
            for n, (which, row) in enumerate(plan[i][0])
        ]

    def store(i):
        which, at, across = plan[i][1]
        block = pl.ds(at, HID)
        return pltpu.make_async_copy(stage.at[i], rest[which].at[:, block] if across else rest[which].at[block], out_sem.at[i])

    for i in range(len(plan)):
        for copy in fetch(i):
            copy.start()
    for i in range(len(plan)):
        for copy in fetch(i):
            copy.wait()
        stage[i] = sum(into[i, n].astype(wide) for n in range(len(plan[i][0]))).astype(low)
        store(i).start()
    for i in range(len(plan)):
        store(i).wait()


def add_call(scalars, arrays, shapes, plan):
    far = pl.BlockSpec(memory_space=pl.ANY)
    blocks, terms = len(plan), len(plan[0][0])
    dma = pltpu.SemaphoreType.DMA
    return pl.pallas_call(
        functools.partial(add_body, len(arrays), plan),
        out_shape=[jax.ShapeDtypeStruct(shape, low) for shape in shapes],
        in_specs=[pl.BlockSpec(memory_space=pltpu.SMEM)] + [far] * len(arrays),
        out_specs=[far] * len(shapes),
        scratch_shapes=[
            pltpu.VMEM((blocks, terms, HID, HID), low),
            pltpu.VMEM((blocks, HID, HID), low),
            dma((blocks, terms)),
            dma((blocks,)),
        ],
        compiler_params=pltpu.CompilerParams(vmem_limit_bytes=60 << 20),
        cost_estimate=pl.CostEstimate(flops=0, bytes_accessed=0, transcendentals=0),
    )(scalars, *arrays)


def sum_body(me, r0, r1, r2, r3, keep, away, total):
    total[...] = r0[0].astype(wide) + r1[0].astype(wide) + r2[0].astype(wide) + r3[0].astype(wide)
    for d in range(4):
        pair = ((me[1] // 2 + d) & 3) * 2
        keep[d, 0] = total[pair + (me[1] & 1)]
        away[d, 0] = total[pair + 1 - (me[1] & 1)].astype(low)


def ring_z(block, me):
    up = down = block
    parts = {0: block}
    for step in (1, 2, 3):
        up, down = shift(up, "z", 1), shift(down, "z", -1)
        parts[step], parts[8 - step] = up, down
    half = NEAR // 2 // 16 * 16
    parts[4] = jnp.concatenate([shift(up[:, :half], "z", 1), shift(down[:, half:], "z", -1)], axis=1)
    buffer = jnp.zeros((2, 8, *block.shape[1:]), low)
    for k, part in parts.items():
        buffer = lax.dynamic_update_slice_in_dim(buffer, part[:, None], (me - k) & 7, 1)
    return buffer


def per_device(patches, proj_in, proj_out, cotangent):
    me = {axis: lax.axis_index(axis) for axis in AXES}
    scalars = jnp.stack([me["x"], me["z"], me["yl"], me["yh"], me["core"]]).astype(jnp.int32)

    both = jnp.concatenate([patches.T, cotangent.T], axis=0)
    near = shift(both, "yl", 1)
    pair = jnp.where(me["yl"] == 0, jnp.stack([both, near]), jnp.stack([near, both]))
    x_pair, c_pair = pair[:, :OWN], pair[:, OWN:]

    c_pair = jnp.concatenate([c_pair, x_pair[:, NEAR:]], axis=1)
    c_parts = [c_pair] + [shift(c_pair, "x", k) for k in range(1, 4)]
    c_x = jnp.concatenate(c_parts, axis=0)
    c_all = lax.all_gather(c_x.reshape(8 * FAR, TOK), "z", axis=0, tiled=True).reshape(8, 4, 2, FAR, TOK)
    x_z = ring_z(x_pair[:, :NEAR], me["z"])
    x_all = [x_z] + [shift(x_z, "x", k) for k in range(1, 4)]

    col_sum = jnp.sum(proj_in.astype(wide), axis=0, keepdims=True)

    dma = pltpu.SemaphoreType.DMA
    near, far = pl.BlockSpec(memory_space=pltpu.VMEM), pl.BlockSpec(memory_space=pl.ANY)
    both_rows = 2 * QUARTER
    shapes = [(2, 8, NEAR, TOK)] * 4 + [(8, 2, 4, FAR, TOK), (8, BLOCK, TOK), (HID, TOK), (TOK, HID)]
    params = pltpu.CompilerParams(vmem_limit_bytes=60 << 20)
    *mlp_parts, patch_parts, norm, act_t, grad = pl.pallas_call(
        main_body,
        out_shape=[jax.ShapeDtypeStruct(shape, low) for shape in shapes],
        in_specs=[pl.BlockSpec(memory_space=pltpu.SMEM)] + [far] * 4 + [near] + [far] * 3,
        out_specs=[far] * len(shapes),
        scratch_shapes=[
            pltpu.VMEM((8, 8, OWN, TOK), low),
            pltpu.VMEM((8, BLOCK, HID), low),
            pltpu.VMEM((8, HID, BLOCK), low),
            pltpu.VMEM((8, 8, OWN, TOK), low),
            pltpu.VMEM((8, BLOCK, TOK), low),
            pltpu.VMEM((8, 8, NEAR, TOK), low),
            pltpu.VMEM((8, 8, REST, TOK), low),
            pltpu.VMEM((8, 8, OWN, TOK), low),
            pltpu.VMEM((HID, TOK), low),
            pltpu.VMEM((TOK, HID), low),
            pltpu.VMEM((TOK, HID), wide),
            pltpu.VMEM((HID, TOK), wide),
        ]
        + [dma((8,))] * 8
        + [dma((3,))],
        compiler_params=params,
        cost_estimate=pl.CostEstimate(flops=6 * work, bytes_accessed=31 << 20, transcendentals=0),
    )(scalars, *x_all, col_sum, proj_in, proj_out, c_all)

    mine, other, away_mine, away_other = pl.pallas_call(
        weights_body,
        out_shape=[jax.ShapeDtypeStruct((both_rows, HID), low)] * 4,
        in_specs=[pl.BlockSpec(memory_space=pltpu.SMEM)] + [far] * 4,
        out_specs=[far] * 4,
        scratch_shapes=[
            pltpu.VMEM((8, 8, OWN, TOK), low),
            pltpu.VMEM((4, 2, BLOCK, TOK), low),
            pltpu.VMEM((HID, TOK), low),
            pltpu.VMEM((TOK, HID), low),
            pltpu.VMEM((4, both_rows, HID), low),
            dma((8,)),
            dma((4,)),
            dma((2,)),
            dma((4,)),
        ],
        compiler_params=params,
        cost_estimate=pl.CostEstimate(flops=2 * work, bytes_accessed=16 << 20, transcendentals=0),
    )(scalars, c_all, norm, act_t, grad)

    got_other = shift(away_other, "core", 1)
    got_mine = shift(away_mine, "core", 1)


    starts = range(0, both_rows, HID)
    head, tail = starts[:2], starts[2:]
    (send,) = add_call(
        scalars,
        [other, got_other],
        [(len(head) * HID, HID)],
        [([(0, row), (1, row)], (0, row, False)) for row in head],
    )
    backs = [shift(send, "yh", 1)]
    send, both_mine = add_call(
        scalars,
        [other, got_other, mine, got_mine],
        [(len(tail) * HID, HID), (both_rows, HID)],
        [([(0, row), (1, row)], (0, row - tail[0], False)) for row in tail]
        + [([(2, row), (3, row)], (1, row, False)) for row in starts],
    )
    backs.append(shift(send, "yh", 1))

    mlp_got = [mlp_parts[0]] + [shift(mlp_parts[k], "x", k) for k in range(1, 4)]
    keep, flip = call(
        sum_body,
        2,
        scalars,
        [(part, pl.BlockSpec((1, 8, NEAR, TOK), lambda t, me: (t, 0, 0, 0))) for part in mlp_got],
        [((4, 2, NEAR, TOK), kind, pl.BlockSpec((4, 1, NEAR, TOK), lambda t, me: (0, t, 0, 0))) for kind in (wide, low)],
        [pltpu.VMEM((8, NEAR, TOK), wide)],
        after=[both_mine[:16, :128], backs[0]],
    )
    keep = keep + lax.ppermute(flip, "z", [(i, i ^ 1) for i in range(8)]).astype(wide)
    total = keep[0]
    for d in range(1, 4):
        total = total + shift(keep[d].astype(low), "z", 2 * d).astype(wide)

    rest = lax.psum_scatter(patch_parts.reshape(64 * FAR, TOK), "z", scatter_dimension=0, tiled=True)
    rest = rest.reshape(2, 4, FAR, TOK)
    rest_total = lax.dynamic_index_in_dim(rest, me["x"], 1, keepdims=False).astype(wide)
    for k in range(1, 4):
        block = lax.dynamic_index_in_dim(rest, (me["x"] + k) & 3, 1, keepdims=False)
        rest_total = rest_total + shift(block, "x", k).astype(wide)

    total = jnp.concatenate([rest_total, total], axis=1)
    mine_y = jnp.where(me["yl"] == 0, total[0], total[1])
    other_y = jnp.where(me["yl"] == 0, total[1], total[0])
    result = (mine_y + shift(other_y.astype(low), "yl", 1).astype(wide)).astype(low)
    patch_grad = result[:OWN].T
    mlp_out = jnp.concatenate([result[FAR:], result[OWN:FAR]], axis=0).T

    plan = []
    for i, row in enumerate(starts):
        back = (1, row) if i < 2 else (2, row - tail[0])
        plan.append(([(0, row), back], (i // 4, i % 4 * HID, i > 3)))
    grad_in, grad_out = add_call(scalars, [both_mine, *backs], [(QUARTER, HID), (HID, QUARTER)], plan)
    return mlp_out, patch_grad, grad_in, grad_out


def solution(mesh):
    devices = np.asarray(mesh.devices).reshape([SIZE[axis] for axis in AXES])
    fine = Mesh(devices, AXES)
    dp, mp = ("yh", "core"), ("yl", "x", "z")
    in_specs = (P(dp, mp), P(None, mp), P(mp, None), P(dp, mp))
    out_specs = (P(dp, mp), P(dp, mp), P(dp, mp), P(mp, dp))
    return jax.shard_map(per_device, mesh=fine, in_specs=in_specs, out_specs=out_specs, check_vma=False)
```

```python
import functools
import math

import jax
import jax.numpy as jnp
import numpy as np
from jax import lax
from jax.experimental import pallas as pl
from jax.experimental.pallas import tpu as pltpu
from jax.sharding import Mesh, PartitionSpec as P

eps = 1e-06
AXES = ("yh", "core", "yl", "x", "z")
SIZE = {"yh": 2, "core": 2, "yl": 2, "x": 4, "z": 8}
low = jnp.bfloat16
wide = jnp.float32
TOK, OWN, HID, WIDTH = 256, 96, 384, 6144
HALF, BLOCK, QUARTER = WIDTH // 2, WIDTH // 8, WIDTH // 4
NEAR = 80
REST = OWN - NEAR
FAR = OWN + REST
root = math.sqrt(2.0 / math.pi)
work = 2 * TOK * WIDTH * HID


def shift(values, axis, step):
    count = SIZE[axis]
    return lax.ppermute(values, axis, [(i, (i + step) % count) for i in range(count)])


def dot(first, second, one, two):
    return lax.dot_general(first, second, (((one,), (two,)), ((), ())), preferred_element_type=wide)


def whole(shape):
    return pl.BlockSpec(shape, lambda t, me: (0,) * len(shape))


def call(body, steps, scalars, ins, outs, scratch=(), after=(), flops=work):
    count = 1 + len(ins)

    def run(*refs):
        body(*refs[:count], *refs[count + len(after) :])

    shapes = [jax.ShapeDtypeStruct(shape, kind) for shape, kind, _ in outs]
    moved = sum(math.prod(v.shape) * v.dtype.itemsize for v in [*(a for a, _ in ins), *shapes])
    return pl.pallas_call(
        run,
        out_shape=shapes,
        grid_spec=pltpu.PrefetchScalarGridSpec(
            num_scalar_prefetch=1,
            grid=(steps,),
            in_specs=[spec for _, spec in ins] + [pl.BlockSpec(memory_space=pl.ANY) for _ in after],
            out_specs=[spec for _, _, spec in outs],
            scratch_shapes=list(scratch),
        ),
        compiler_params=pltpu.CompilerParams(vmem_limit_bytes=24 << 20),
        cost_estimate=pl.CostEstimate(flops=flops, bytes_accessed=moved, transcendentals=0),
    )(scalars, *(a for a, _ in ins), *after)


def block_at(me, k, yl):
    return yl * 4 + ((me[0] - k) & 3)


def rows_of(block):
    return pl.ds(pl.multiple_of(block * BLOCK, BLOCK), BLOCK)


def gelu_parts(hidden):
    square = hidden * hidden
    tanh = jnp.tanh(root * (hidden + 0.044715 * hidden * square))
    half = 0.5 * (1.0 + tanh)
    slope = half + 0.5 * hidden * (1.0 - tanh * tanh) * (root * (1.0 + 3 * 0.044715 * square))
    return hidden * half, slope


def main_body(me, p0, p1, p2, p3, col_sum, w_in, w_out, part, *refs):
    mlp_outs, (patch, norm_out, act_out, grad_out) = refs[:4], refs[4:8]
    p_near, in_near, out_near, cot, norm, mlp_stage, rest_stage, patch_stage, act_near, grad_near, acc, grad_acc = refs[8:20]
    p_sem, rest_sem, in_sem, out_sem, cot_sem, mlp_sem, mlp_rest_sem, patch_sem, extra_sem = refs[20:]
    first_rows, rest_rows, far_rows = pl.ds(0, NEAR), pl.ds(NEAR, REST), pl.ds(OWN, REST)

    def p_copy(t, piece, yl):
        return pltpu.make_async_copy(piece.at[yl], p_near.at[t, :, first_rows], p_sem.at[t])

    def rest_copy(t):
        source = part.at[:, t // 2, t % 2, far_rows]
        return pltpu.make_async_copy(source, p_near.at[t, :, rest_rows], rest_sem.at[t])

    def in_copy(t):
        return pltpu.make_async_copy(w_in.at[rows_of(block_at(me, t // 2, t % 2))], in_near.at[t], in_sem.at[t])

    def out_copy(j):
        return pltpu.make_async_copy(w_out.at[:, rows_of(j)], out_near.at[j], out_sem.at[j])

    def cot_copy(j):
        source = part.at[:, (me[0] - (j % 4)) & 3, j // 4, pl.ds(0, OWN)]
        return pltpu.make_async_copy(source, cot.at[j], cot_sem.at[j])

    for t in range(8):
        p_copy(t, (p0, p1, p2, p3)[t // 2], t % 2).start()
        rest_copy(t).start()
    for t in range(8):
        in_copy(t).start()
    acc[...] = jnp.zeros_like(acc)
    grad_acc[...] = jnp.zeros_like(grad_acc)

    def sums_step(t, sums):
        p_copy(t, p0, 0).wait()
        rest_copy(t).wait()
        value = p_near[t].reshape(BLOCK, TOK).astype(wide)
        return sums[0] + jnp.sum(value, axis=0, keepdims=True), sums[1] + jnp.sum(value * value, axis=0, keepdims=True)

    zero = jnp.zeros((1, TOK), wide)
    sums = lax.fori_loop(0, 8, sums_step, (zero, zero))
    for j in range(8):
        out_copy(j).start()
        cot_copy(j).start()
    mean = sums[0] / WIDTH
    rstd = lax.rsqrt(sums[1] / WIDTH - mean * mean + eps)

    def hidden_step(t, _):
        value = ((p_near[t].reshape(BLOCK, TOK).astype(wide) - mean) * rstd).astype(low)
        norm[block_at(me, t // 2, t % 2)] = value
        in_copy(t).wait()
        acc[...] += dot(value, in_near[t], 0, 0)
        return 0

    lax.fori_loop(0, 8, hidden_step, 0)

    def grad_step(j, _):
        out_copy(j).wait()
        cot_copy(j).wait()
        grad_acc[...] += dot(out_near[j], cot[j].reshape(BLOCK, TOK), 1, 0)
        return 0

    lax.fori_loop(0, 8, grad_step, 0)

    hidden = acc[...].T
    act_wide, slope = gelu_parts(hidden)
    act_t = act_wide.astype(low)
    act = act_wide.T.astype(low)
    grad_wide = slope * grad_acc[...]
    grad_t = grad_wide.astype(low)
    grad = grad_wide.T.astype(low)
    rounded = grad_t.astype(wide)
    first = jnp.sum(rounded * col_sum[...].T, axis=0, keepdims=True) / WIDTH
    second = jnp.sum(rounded * hidden, axis=0, keepdims=True) / WIDTH

    act_near[...] = act_t
    grad_near[...] = grad
    extra = [
        pltpu.make_async_copy(source, to, extra_sem.at[i])
        for i, (source, to) in enumerate(((norm, norm_out), (act_near, act_out), (grad_near, grad_out)))
    ]
    for copy in extra:
        copy.start()

    def patch_copy(t):
        to = patch.at[:, t % 2, (me[0] - t // 2) & 3, pl.ds(0, OWN)]
        return pltpu.make_async_copy(patch_stage.at[t], to, patch_sem.at[t])

    def patch_step(t, _):
        share = dot(in_near[t], grad_t, 1, 0)
        normed = (p_near[t].reshape(BLOCK, TOK).astype(wide) - mean) * rstd
        share = rstd * (share - first - normed * second)
        patch_stage[t] = share.astype(low).reshape(8, OWN, TOK)
        patch_copy(t).start()
        return 0

    lax.fori_loop(0, 8, patch_step, 0)

    def mlp_copy(t):
        return pltpu.make_async_copy(mlp_stage.at[t], mlp_outs[t // 2].at[t % 2], mlp_sem.at[t])

    def mlp_rest_copy(t):
        to = patch.at[:, t % 2, (me[0] + t // 2) & 3, far_rows]
        return pltpu.make_async_copy(rest_stage.at[t], to, mlp_rest_sem.at[t])

    for t in range(8):
        value = dot(act, out_near[(t % 2) * 4 + ((me[0] + t // 2) & 3)], 1, 0)
        value = value.T.astype(low).reshape(8, OWN, TOK)
        mlp_stage[t] = value[:, :NEAR]
        mlp_copy(t).start()
        rest_stage[t] = value[:, NEAR:]
        mlp_rest_copy(t).start()
    for t in range(8):
        patch_copy(t).wait()
        mlp_copy(t).wait()
        mlp_rest_copy(t).wait()
    for copy in extra:
        copy.wait()


def weights_body(me, part, norm_in, act_in, grad_in, mine, other, away_mine, away_other, *refs):
    cot, norm, act_near, grad_near, grad_stage, cot_sem, norm_sem, small_sem, grad_sem = refs

    def spot(q):
        yh = me[3] if q in (1, 3) else 1 - me[3]
        return (yh * 2 + (1 - me[4] if q < 2 else me[4])) * 2

    def cot_copy(q, i):
        j = spot(q) + i
        source = part.at[:, (me[0] - (j % 4)) & 3, j // 4, pl.ds(0, OWN)]
        return pltpu.make_async_copy(source, cot.at[2 * q + i], cot_sem.at[2 * q + i])

    def norm_copy(q):
        return pltpu.make_async_copy(norm_in.at[pl.ds(spot(q), 2)], norm.at[q], norm_sem.at[q])

    small = [
        pltpu.make_async_copy(grad_in, grad_near, small_sem.at[0]),
        pltpu.make_async_copy(act_in, act_near, small_sem.at[1]),
    ]
    for copy in small:
        copy.start()
    for q in range(4):
        norm_copy(q).start()
        cot_copy(q, 0).start()
        cot_copy(q, 1).start()
    for copy in small:
        copy.wait()
    grad, act_t = grad_near[...], act_near[...]

    grad_to = (away_other, away_mine, other, mine)

    def grad_copy(q):
        return pltpu.make_async_copy(grad_stage.at[q], grad_to[q], grad_sem.at[q])

    for q in range(4):
        norm_copy(q).wait()
        grad_stage[q, :QUARTER] = dot(norm[q].reshape(QUARTER, TOK), grad, 1, 0).astype(low)
        cot_copy(q, 0).wait()
        cot_copy(q, 1).wait()
        value = dot(act_t, cot[2 * q : 2 * q + 2].reshape(QUARTER, TOK), 1, 1).astype(low)
        for i in range(4):
            grad_stage[q, QUARTER + i * HID : QUARTER + (i + 1) * HID] = value[:, i * HID : (i + 1) * HID]
        grad_copy(q).start()
    for q in range(4):
        grad_copy(q).wait()


def add_body(count, plan, me, *refs):
    ins, rest = refs[:count], refs[count:]
    into, stage, in_sem, out_sem = rest[-4:]

    def fetch(i):
        return [
            pltpu.make_async_copy(ins[which].at[pl.ds(row, HID)], into.at[i, n], in_sem.at[i, n])
            for n, (which, row) in enumerate(plan[i][0])
        ]

    def store(i):
        which, at, across = plan[i][1]
        block = pl.ds(at, HID)
        return pltpu.make_async_copy(stage.at[i], rest[which].at[:, block] if across else rest[which].at[block], out_sem.at[i])

    for i in range(len(plan)):
        for copy in fetch(i):
            copy.start()
    for i in range(len(plan)):
        for copy in fetch(i):
            copy.wait()
        stage[i] = sum(into[i, n].astype(wide) for n in range(len(plan[i][0]))).astype(low)
        store(i).start()
    for i in range(len(plan)):
        store(i).wait()


def add_call(scalars, arrays, shapes, plan):
    far = pl.BlockSpec(memory_space=pl.ANY)
    blocks, terms = len(plan), len(plan[0][0])
    dma = pltpu.SemaphoreType.DMA
    return pl.pallas_call(
        functools.partial(add_body, len(arrays), plan),
        out_shape=[jax.ShapeDtypeStruct(shape, low) for shape in shapes],
        in_specs=[pl.BlockSpec(memory_space=pltpu.SMEM)] + [far] * len(arrays),
        out_specs=[far] * len(shapes),
        scratch_shapes=[
            pltpu.VMEM((blocks, terms, HID, HID), low),
            pltpu.VMEM((blocks, HID, HID), low),
            dma((blocks, terms)),
            dma((blocks,)),
        ],
        compiler_params=pltpu.CompilerParams(vmem_limit_bytes=60 << 20),
        cost_estimate=pl.CostEstimate(flops=0, bytes_accessed=0, transcendentals=0),
    )(scalars, *arrays)


def sum_body(me, r0, r1, r2, r3, keep, away, total):
    total[...] = r0[0].astype(wide) + r1[0].astype(wide) + r2[0].astype(wide) + r3[0].astype(wide)
    for d in range(4):
        pair = ((me[1] // 2 + d) & 3) * 2
        keep[d, 0] = total[pair + (me[1] & 1)]
        away[d, 0] = total[pair + 1 - (me[1] & 1)].astype(low)


def ring_z(block, me):
    up = down = block
    parts = {0: block}
    for step in (1, 2, 3):
        up, down = shift(up, "z", 1), shift(down, "z", -1)
        parts[step], parts[8 - step] = up, down
    half = NEAR // 2 // 16 * 16
    parts[4] = jnp.concatenate([shift(up[:, :half], "z", 1), shift(down[:, half:], "z", -1)], axis=1)
    buffer = jnp.zeros((2, 8, *block.shape[1:]), low)
    for k, part in parts.items():
        buffer = lax.dynamic_update_slice_in_dim(buffer, part[:, None], (me - k) & 7, 1)
    return buffer


def per_device(patches, proj_in, proj_out, cotangent):
    me = {axis: lax.axis_index(axis) for axis in AXES}
    scalars = jnp.stack([me["x"], me["z"], me["yl"], me["yh"], me["core"]]).astype(jnp.int32)

    both = jnp.concatenate([patches.T, cotangent.T], axis=0)
    near = shift(both, "yl", 1)
    pair = jnp.where(me["yl"] == 0, jnp.stack([both, near]), jnp.stack([near, both]))
    x_pair, c_pair = pair[:, :OWN], pair[:, OWN:]

    c_pair = jnp.concatenate([c_pair, x_pair[:, NEAR:]], axis=1)
    c_parts = [c_pair] + [shift(c_pair, "x", k) for k in range(1, 4)]
    c_x = jnp.concatenate(c_parts, axis=0)
    c_all = lax.all_gather(c_x.reshape(8 * FAR, TOK), "z", axis=0, tiled=True).reshape(8, 4, 2, FAR, TOK)
    x_z = ring_z(x_pair[:, :NEAR], me["z"])
    x_all = [x_z] + [shift(x_z, "x", k) for k in range(1, 4)]

    col_sum = jnp.sum(proj_in.astype(wide), axis=0, keepdims=True)

    dma = pltpu.SemaphoreType.DMA
    near, far = pl.BlockSpec(memory_space=pltpu.VMEM), pl.BlockSpec(memory_space=pl.ANY)
    both_rows = 2 * QUARTER
    shapes = [(2, 8, NEAR, TOK)] * 4 + [(8, 2, 4, FAR, TOK), (8, BLOCK, TOK), (HID, TOK), (TOK, HID)]
    params = pltpu.CompilerParams(vmem_limit_bytes=60 << 20)
    *mlp_parts, patch_parts, norm, act_t, grad = pl.pallas_call(
        main_body,
        out_shape=[jax.ShapeDtypeStruct(shape, low) for shape in shapes],
        in_specs=[pl.BlockSpec(memory_space=pltpu.SMEM)] + [far] * 4 + [near] + [far] * 3,
        out_specs=[far] * len(shapes),
        scratch_shapes=[
            pltpu.VMEM((8, 8, OWN, TOK), low),
            pltpu.VMEM((8, BLOCK, HID), low),
            pltpu.VMEM((8, HID, BLOCK), low),
            pltpu.VMEM((8, 8, OWN, TOK), low),
            pltpu.VMEM((8, BLOCK, TOK), low),
            pltpu.VMEM((8, 8, NEAR, TOK), low),
            pltpu.VMEM((8, 8, REST, TOK), low),
            pltpu.VMEM((8, 8, OWN, TOK), low),
            pltpu.VMEM((HID, TOK), low),
            pltpu.VMEM((TOK, HID), low),
            pltpu.VMEM((TOK, HID), wide),
            pltpu.VMEM((HID, TOK), wide),
        ]
        + [dma((8,))] * 8
        + [dma((3,))],
        compiler_params=params,
        cost_estimate=pl.CostEstimate(flops=6 * work, bytes_accessed=31 << 20, transcendentals=0),
    )(scalars, *x_all, col_sum, proj_in, proj_out, c_all)

    mine, other, away_mine, away_other = pl.pallas_call(
        weights_body,
        out_shape=[jax.ShapeDtypeStruct((both_rows, HID), low)] * 4,
        in_specs=[pl.BlockSpec(memory_space=pltpu.SMEM)] + [far] * 4,
        out_specs=[far] * 4,
        scratch_shapes=[
            pltpu.VMEM((8, 8, OWN, TOK), low),
            pltpu.VMEM((4, 2, BLOCK, TOK), low),
            pltpu.VMEM((HID, TOK), low),
            pltpu.VMEM((TOK, HID), low),
            pltpu.VMEM((4, both_rows, HID), low),
            dma((8,)),
            dma((4,)),
            dma((2,)),
            dma((4,)),
        ],
        compiler_params=params,
        cost_estimate=pl.CostEstimate(flops=2 * work, bytes_accessed=16 << 20, transcendentals=0),
    )(scalars, c_all, norm, act_t, grad)

    got_other = shift(away_other, "core", 1)
    got_mine = shift(away_mine, "core", 1)


    starts = range(0, both_rows, HID)
    head, tail = starts[:2], starts[2:]
    (send,) = add_call(
        scalars,
        [other, got_other],
        [(len(head) * HID, HID)],
        [([(0, row), (1, row)], (0, row, False)) for row in head],
    )
    backs = [shift(send, "yh", 1)]
    send, both_mine = add_call(
        scalars,
        [other, got_other, mine, got_mine],
        [(len(tail) * HID, HID), (both_rows, HID)],
        [([(0, row), (1, row)], (0, row - tail[0], False)) for row in tail]
        + [([(2, row), (3, row)], (1, row, False)) for row in starts],
    )
    backs.append(shift(send, "yh", 1))

    mlp_got = [mlp_parts[0]] + [shift(mlp_parts[k], "x", k) for k in range(1, 4)]
    keep, flip = call(
        sum_body,
        2,
        scalars,
        [(part, pl.BlockSpec((1, 8, NEAR, TOK), lambda t, me: (t, 0, 0, 0))) for part in mlp_got],
        [((4, 2, NEAR, TOK), kind, pl.BlockSpec((4, 1, NEAR, TOK), lambda t, me: (0, t, 0, 0))) for kind in (wide, low)],
        [pltpu.VMEM((8, NEAR, TOK), wide)],
        after=[both_mine[:16, :128], backs[0]],
    )
    keep = keep + lax.ppermute(flip, "z", [(i, i ^ 1) for i in range(8)]).astype(wide)
    total = keep[0]
    for d in range(1, 4):
        total = total + shift(keep[d].astype(low), "z", 2 * d).astype(wide)

    rest = lax.psum_scatter(patch_parts.reshape(64 * FAR, TOK), "z", scatter_dimension=0, tiled=True)
    rest = rest.reshape(2, 4, FAR, TOK)
    rest_total = lax.dynamic_index_in_dim(rest, me["x"], 1, keepdims=False).astype(wide)
    for k in range(1, 4):
        block = lax.dynamic_index_in_dim(rest, (me["x"] + k) & 3, 1, keepdims=False)
        rest_total = rest_total + shift(block, "x", k).astype(wide)

    total = jnp.concatenate([rest_total, total], axis=1)
    mine_y = jnp.where(me["yl"] == 0, total[0], total[1])
    other_y = jnp.where(me["yl"] == 0, total[1], total[0])
    result = (mine_y + shift(other_y.astype(low), "yl", 1).astype(wide)).astype(low)
    patch_grad = result[:OWN].T
    mlp_out = jnp.concatenate([result[FAR:], result[OWN:FAR]], axis=0).T

    plan = []
    for i, row in enumerate(starts):
        back = (1, row) if i < 2 else (2, row - tail[0])
        plan.append(([(0, row), back], (i // 4, i % 4 * HID, i > 3)))
    grad_in, grad_out = add_call(scalars, [both_mine, *backs], [(QUARTER, HID), (HID, QUARTER)], plan)
    return mlp_out, patch_grad, grad_in, grad_out


def solution(mesh):
    devices = np.asarray(mesh.devices).reshape([SIZE[axis] for axis in AXES])
    fine = Mesh(devices, AXES)
    dp, mp = ("yh", "core"), ("yl", "x", "z")
    in_specs = (P(dp, mp), P(None, mp), P(mp, None), P(dp, mp))
    out_specs = (P(dp, mp), P(dp, mp), P(dp, mp), P(mp, dp))
    return jax.shard_map(per_device, mesh=fine, in_specs=in_specs, out_specs=out_specs, check_vma=False)
```
